512 devices in a mesh: rep: 16 (over z_hi, y), fsdp: 8 (over z_lo, core), tp: 4 (over x).
Axes of the slice: x: 4, y: 4, z: 16 (z_hi: 4, z_lo: 4; z = z_hi * 4 + z_lo), core: 2. Of those that a mesh axis runs over, the one named last changes fastest.
Arguments:
- partner: int32 [3, 16], replicated, may hold values from 0 to 15, as said below
- weight_gate: float32 [16, 128, 25600], P('rep', 'fsdp', 'tp'), may hold values from -6 to 6
- weight_up: float32 [16, 128, 25600], P('rep', 'fsdp', 'tp'), may hold values from -6 to 6
- weight_down: float32 [16, 128, 5120], P('rep', 'fsdp', 'tp'), may hold values from -6 to 6
- moment_gate: float32 [16, 128, 25600], P('rep', 'fsdp', 'tp'), may hold values from -6 to 6
- moment_up: float32 [16, 128, 25600], P('rep', 'fsdp', 'tp'), may hold values from -6 to 6
- moment_down: float32 [16, 128, 5120], P('rep', 'fsdp', 'tp'), may hold values from -6 to 6
- grad_gate: bfloat16 [16, 128, 25600], P('rep', 'fsdp', 'tp')
- grad_up: bfloat16 [16, 128, 25600], P('rep', 'fsdp', 'tp')
- grad_down: bfloat16 [16, 128, 5120], P('rep', 'fsdp', 'tp')
Outputs:
- new_weight_gate: float32 [16, 128, 25600], P('rep', 'fsdp', 'tp')
- new_weight_up: float32 [16, 128, 25600], P('rep', 'fsdp', 'tp')
- new_weight_down: float32 [16, 128, 5120], P('rep', 'fsdp', 'tp')
- new_moment_gate: float32 [16, 128, 25600], P('rep', 'fsdp', 'tp')
- new_moment_up: float32 [16, 128, 25600], P('rep', 'fsdp', 'tp')
- new_moment_down: float32 [16, 128, 5120], P('rep', 'fsdp', 'tp')
The draws below stay inside these ranges and needn't reach their ends.
Inputs may be any that keep to these rules, and one draw needn't show every extreme that they name: Each row of partner is a matching: partner[m, partner[m, r]] = r and partner[m, r] != r for every replica r.
All inputs are finite; a program needn't handle non-finite values.
Results may differ from the reference program's by a relative error of at most 0.0003.
Values may be sent and summed in bfloat16 or wider, within the bound.
No kernel may reach another device: no remote copies, remote signals or barrier semaphores. Data moves between devices by JAX's collectives and lax.ppermute only.
A program may use at most 64 MiB of HBM per device.

```python
import math
import jax
import jax.numpy as jnp
from jax import lax

D = 5120
FF = 25600
REPLICAS = 16
GATE_ROWS = 128
DOWN_ROWS = 128


def envelope(key, array_shape, row_span):
    key_rows, key_jitter = jax.random.split(key, 2)
    rows = array_shape[1]
    cols = array_shape[2]
    row_rise = jnp.exp(math.log(3.0) * jnp.arange(rows, dtype=jnp.float32) / rows)
    col_rise = jnp.exp(math.log(3.0) * jnp.arange(cols, dtype=jnp.float32) / cols)
    row_gain = jnp.exp(jax.random.uniform(key_rows, (array_shape[0], rows, 1), jnp.float32, 0.0, row_span))
    jitter = jnp.exp(jax.random.uniform(key_jitter, array_shape, jnp.float32, 0.0, 0.7))
    return row_gain * row_rise[None, :, None] * col_rise[None, None, :] * jitter


def one_matching(key):
    order = jax.random.permutation(key, REPLICAS).astype(jnp.int32)
    firsts = order[0::2]
    seconds = order[1::2]
    mates = jnp.zeros((REPLICAS,), jnp.int32)
    mates = mates.at[firsts].set(seconds)
    mates = mates.at[seconds].set(firsts)
    return mates


def draw_partner(key, part):
    key = jax.random.fold_in(key, 5)
    keys = jax.random.split(key, 3)
    return jnp.stack([one_matching(keys[0]), one_matching(keys[1]), one_matching(keys[2])], axis=0)


def draw_grad_gate(key, part):
    key = jax.random.fold_in(key, 11)
    key_noise = jax.random.fold_in(key, 0)
    key_scale = jax.random.fold_in(key, 2)
    array_shape = (REPLICAS, GATE_ROWS, FF)
    noise_base = jax.random.normal(key_noise, array_shape, jnp.float32)
    scale_field = envelope(key_scale, array_shape, math.log(10.0))
    return (noise_base * scale_field).astype(jnp.bfloat16)


def draw_grad_up(key, part):
    key = jax.random.fold_in(key, 23)
    key_noise = jax.random.fold_in(key, 0)
    key_scale = jax.random.fold_in(key, 2)
    array_shape = (REPLICAS, GATE_ROWS, FF)
    noise_base = jax.random.normal(key_noise, array_shape, jnp.float32)
    scale_field = envelope(key_scale, array_shape, math.log(10.0))
    return (noise_base * scale_field).astype(jnp.bfloat16)


def draw_grad_down(key, part):
    key = jax.random.fold_in(key, 37)
    key_noise = jax.random.fold_in(key, 0)
    key_scale = jax.random.fold_in(key, 2)
    array_shape = (REPLICAS, DOWN_ROWS, D)
    noise_base = jax.random.normal(key_noise, array_shape, jnp.float32)
    scale_field = envelope(key_scale, array_shape, math.log(10.0))
    return (noise_base * scale_field).astype(jnp.bfloat16)


def levels(own_key, dims, cuts, low, high):
    gain = 1.0
    for dim, blocks in cuts:
        draws = jax.random.uniform(jax.random.fold_in(jax.random.fold_in(own_key, 6), dim), (blocks,), jnp.float32, low / len(cuts), high / len(cuts))
        gain = gain * jnp.repeat(jnp.exp(draws), dims[dim] // blocks).reshape((-1,) + (1,) * (len(dims) - 1 - dim))
    return gain


def centred(stream_key, shape, width, bound, cuts=(), kind=jnp.bfloat16):
    values = jax.random.normal(stream_key, shape, jnp.float32) * width
    if len(cuts) > 0:
        values = levels(stream_key, shape, cuts, -0.22, 0.18) * values
    return jnp.clip(values, min=-bound, max=bound).astype(kind)


def setup_inputs(seed: int = 0) -> dict:
    key_list = jax.random.split(jax.random.key(seed), 11)
    partner = draw_partner(jax.random.fold_in(key_list[10], 71), 0)
    weight_gate = centred(key_list[1], (REPLICAS, GATE_ROWS, FF), 1.0, 6.0, ((0, 16), (1, 8), (2, 4)), jnp.float32)
    weight_up = centred(key_list[2], (REPLICAS, GATE_ROWS, FF), 1.0, 6.0, ((0, 16), (1, 8), (2, 4)), jnp.float32)
    weight_down = centred(key_list[3], (REPLICAS, DOWN_ROWS, D), 1.0, 6.0, ((0, 16), (1, 8), (2, 4)), jnp.float32)
    moment_gate = centred(key_list[4], (REPLICAS, GATE_ROWS, FF), 1.0, 6.0, ((0, 16), (1, 8), (2, 4)), jnp.float32)
    moment_up = centred(key_list[5], (REPLICAS, GATE_ROWS, FF), 1.0, 6.0, ((0, 16), (1, 8), (2, 4)), jnp.float32)
    moment_down = centred(key_list[6], (REPLICAS, DOWN_ROWS, D), 1.0, 6.0, ((0, 16), (1, 8), (2, 4)), jnp.float32)
    grad_gate = draw_grad_gate(jax.random.fold_in(key_list[10], 71), 0)
    grad_up = draw_grad_up(jax.random.fold_in(key_list[10], 71), 0)
    grad_down = draw_grad_down(jax.random.fold_in(key_list[10], 71), 0)
    return dict(partner=partner, weight_gate=weight_gate, weight_up=weight_up, weight_down=weight_down, moment_gate=moment_gate, moment_up=moment_up, moment_down=moment_down, grad_gate=grad_gate, grad_up=grad_up, grad_down=grad_down)


CLIP_RATIO = 0.5
BETA = 0.9
GAMMA = 0.4
RATE = 0.7
EPS = 1e-06

def outer_update(weight, moment, grad, mates):
    mate_grad = jnp.take(grad, mates, axis=0)
    mate_weight = jnp.take(weight, mates, axis=0)
    mixed = 0.5 * (grad.astype(jnp.float32) + mate_grad.astype(jnp.float32))
    squares = lax.optimization_barrier(jnp.sum(jnp.square(mixed), axis=(1, 2), keepdims=True))
    clip_bound = CLIP_RATIO * jnp.sqrt(jnp.float32(weight.shape[1] * weight.shape[2]))
    clip_factor = jnp.minimum(1.0, clip_bound / jnp.sqrt(squares + EPS))
    scaled = clip_factor * mixed
    new_moment = BETA * moment + scaled
    new_weight = weight - GAMMA * (weight - mate_weight) - RATE * (scaled + BETA * new_moment)
    return (new_weight, new_moment)

def reference(partner, weight_gate, weight_up, weight_down, moment_gate, moment_up, moment_down, grad_gate, grad_up, grad_down):
    new_gate, mom_gate = outer_update(weight_gate, moment_gate, grad_gate, partner[0])
    new_up, mom_up = outer_update(weight_up, moment_up, grad_up, partner[1])
    new_down, mom_down = outer_update(weight_down, moment_down, grad_down, partner[2])
    return (new_gate, new_up, new_down, mom_gate, mom_up, mom_down)
```

```python
import functools

import jax
import jax.numpy as jnp
from jax import lax
from jax.experimental import pallas as pl
from jax.experimental.pallas import tpu as pltpu
from jax.sharding import PartitionSpec as P

CLIP_RATIO = 0.5
BETA = 0.9
GAMMA = 0.4
RATE = 0.7
EPS = 1e-06

LANES = 128
TOP = 32767.0
STEPS = 16.0
VMEM_LIMIT = 24 * 1024 * 1024


def plan(widths, replicas):
    starts, at = [], 0
    for width in widths:
        count = width // LANES
        starts.append((at, at + count))
        at += 2 * count
    scales = tuple(at + slot for slot in range(3))
    per_home = -(-(at + 3) // replicas)
    return tuple(starts), scales, per_home


def exponent(peak):
    power = jnp.ceil(STEPS * jnp.log2(jnp.maximum(peak, 2.0**-120)))
    return jnp.clip(power, -120.0 * STEPS, 128.0 * STEPS - 1.0)


def encode_kernel(starts, scales, per_home, wg, wu, wd, gg, gu, gd, out):
    rows = wg.shape[1]

    def put(tile, value):
        home, place = divmod(tile, per_home)
        out[home, place * rows : (place + 1) * rows, :] = value

    def coded(block_ref, first):
        count = block_ref.shape[2] // LANES
        peak = jnp.zeros((rows, LANES), jnp.float32)
        for c in range(count):
            peak = jnp.maximum(peak, jnp.abs(block_ref[0, :, c * LANES : (c + 1) * LANES].astype(jnp.float32)))
        power = exponent(jnp.max(peak, axis=(0, 1), keepdims=True))
        factor = jnp.broadcast_to(jnp.exp2(power * (-1.0 / STEPS)), (rows, LANES))
        for c in range(count):
            x = block_ref[0, :, c * LANES : (c + 1) * LANES].astype(jnp.float32)
            level = jnp.minimum(TOP * jnp.sqrt(jnp.abs(x) * factor), TOP) + 0.5
            level = jnp.where(x < 0, -level, level)
            put(first + c, level.astype(jnp.int32).astype(jnp.int16))
        return jnp.broadcast_to(power, (rows, LANES)).astype(jnp.int32)

    upper = lax.broadcasted_iota(jnp.int32, (rows, LANES), 0) < 8
    for slot, (w, g) in enumerate(((wg, gg), (wu, gu), (wd, gd))):
        power_w = coded(w, starts[slot][0])
        power_g = coded(g, starts[slot][1])
        put(scales[slot], jnp.where(upper, power_w, power_g).astype(jnp.int16))
    for tile in range(scales[2] + 1, out.shape[0] * per_home):
        put(tile, jnp.zeros((rows, LANES), jnp.int16))


def swap_kernel(starts, scales, per_home, rows, partner, me, inp, out):
    replicas = inp.shape[0]
    for place in range(per_home):
        tile = me[0] * per_home + place
        slot = jnp.where(tile < starts[1][0], 0, jnp.where(tile < starts[2][0], 1, 2))
        slot = jnp.where(tile == scales[0], 0, jnp.where(tile == scales[1], 1, slot))
        for r in range(replicas):
            source = partner[slot, r]
            out[r, place * rows : (place + 1) * rows, :] = inp[source, place * rows : (place + 1) * rows, :]


def reader(per_home, rows, payload):
    def get(tile):
        home, place = divmod(tile, per_home)
        return payload[home, place * rows : (place + 1) * rows, :].astype(jnp.int32).astype(jnp.float32)

    return get


def decoded(code, scale):
    a = code * (1.0 / TOP)
    return a * jnp.abs(a) * scale


def scales_of(get, tile):
    power = jnp.exp2(get(tile) * (1.0 / STEPS))
    return power[0:1, :], power[8:9, :]


def squares_kernel(starts, scales, per_home, payload, gg, gu, gd, out):
    rows = gg.shape[1]
    get = reader(per_home, rows, payload)
    lane = lax.broadcasted_iota(jnp.int32, (1, LANES), 1)
    total = jnp.zeros((1, LANES), jnp.float32)
    for slot, g in enumerate((gg, gu, gd)):
        _, scale = scales_of(get, scales[slot])
        sums = jnp.zeros((rows, LANES), jnp.float32)
        for c in range(g.shape[2] // LANES):
            own = g[0, :, c * LANES : (c + 1) * LANES].astype(jnp.float32)
            mixed = 0.5 * (own + decoded(get(starts[slot][1] + c), scale))
            sums = sums + mixed * mixed
        total = jnp.where(lane == slot, jnp.sum(sums, axis=(0, 1), keepdims=True), total)
    out[...] = jnp.broadcast_to(total[None], out.shape)


def update_kernel(starts, scales, per_home, elements, sums, payload, wg, wu, wd, mg, mu, md, gg, gu, gd, og, ou, od, ng, nu, nd):
    rows = gg.shape[1]
    get = reader(per_home, rows, payload)
    lane = lax.broadcasted_iota(jnp.int32, (1, LANES), 1)
    totals = jnp.sum(sums[...], axis=0)
    groups = ((wg, mg, gg, og, ng), (wu, mu, gu, ou, nu), (wd, md, gd, od, nd))
    for slot, (w, m, g, o, n) in enumerate(groups):
        scale_w, scale_g = scales_of(get, scales[slot])
        squares = jnp.sum(jnp.where(lane == slot, totals, 0.0), axis=(0, 1), keepdims=True)
        bound = CLIP_RATIO * float(elements[slot]) ** 0.5
        clip = jnp.broadcast_to(jnp.minimum(1.0, bound / jnp.sqrt(squares + EPS)), (rows, LANES))
        for c in range(w.shape[2] // LANES):
            part = slice(c * LANES, (c + 1) * LANES)
            own = g[0, :, part].astype(jnp.float32)
            mixed = 0.5 * (own + decoded(get(starts[slot][1] + c), scale_g))
            mate = decoded(get(starts[slot][0] + c), scale_w)
            scaled = clip * mixed
            moment = BETA * m[0, :, part] + scaled
            weight = w[0, :, part]
            n[0, :, part] = moment
            o[0, :, part] = weight - GAMMA * (weight - mate) - RATE * (scaled + BETA * moment)


def local(partner, wg, wu, wd, mg, mu, md, gg, gu, gd):
    replicas = lax.axis_size("rep")
    shards = lax.axis_size("fsdp") * lax.axis_size("tp")
    rows = wg.shape[1]
    starts, scales, per_home = plan((wg.shape[2], wu.shape[2], wd.shape[2]), replicas)
    params = pltpu.CompilerParams(vmem_limit_bytes=VMEM_LIMIT)
    vmem = pl.BlockSpec(memory_space=pltpu.VMEM)
    smem = pl.BlockSpec(memory_space=pltpu.SMEM)
    packed = jax.ShapeDtypeStruct((replicas, per_home * rows, LANES), jnp.int16)

    coded = pl.pallas_call(
        functools.partial(encode_kernel, starts, scales, per_home),
        out_shape=packed,
        in_specs=[vmem] * 6,
        out_specs=vmem,
        compiler_params=params,
        name="encode",
    )(wg, wu, wd, gg, gu, gd)
    homed = lax.all_to_all(coded, "rep", 0, 0, tiled=True)
    me = lax.axis_index("rep").reshape(1).astype(jnp.int32)
    swapped = pl.pallas_call(
        functools.partial(swap_kernel, starts, scales, per_home, rows),
        out_shape=packed,
        in_specs=[smem, smem, vmem],
        out_specs=vmem,
        compiler_params=params,
        name="swap",
    )(partner, me, homed)
    mates = lax.all_to_all(swapped, "rep", 0, 0, tiled=True)
    partial = pl.pallas_call(
        functools.partial(squares_kernel, starts, scales, per_home),
        out_shape=jax.ShapeDtypeStruct((shards, 1, LANES), jnp.float32),
        in_specs=[vmem] * 4,
        out_specs=vmem,
        compiler_params=params,
        name="squares",
    )(mates, gg, gu, gd)
    sums = lax.all_to_all(partial, ("fsdp", "tp"), 0, 0, tiled=True)
    elements = tuple(shards * w.shape[1] * w.shape[2] for w in (wg, wu, wd))
    arrays = [jax.ShapeDtypeStruct(a.shape, jnp.float32) for a in (wg, wu, wd, mg, mu, md)]
    return pl.pallas_call(
        functools.partial(update_kernel, starts, scales, per_home, elements),
        out_shape=arrays,
        in_specs=[vmem] * 11,
        out_specs=[vmem] * 6,
        compiler_params=params,
        name="update",
    )(sums, mates, wg, wu, wd, mg, mu, md, gg, gu, gd)


def solution(mesh):
    spec = P("rep", "fsdp", "tp")
    return jax.shard_map(
        local,
        mesh=mesh,
        in_specs=(P(),) + (spec,) * 9,
        out_specs=(spec,) * 6,
        check_vma=False,
    )
```

```python
import functools

import jax
import jax.numpy as jnp
from jax import lax
from jax.experimental import pallas as pl
from jax.experimental.pallas import tpu as pltpu
from jax.sharding import PartitionSpec as P

CLIP_RATIO = 0.5
BETA = 0.9
GAMMA = 0.4
RATE = 0.7
EPS = 1e-06

LANES = 128
TOP = 32767.0
STEPS = 16.0
VMEM_LIMIT = 24 * 1024 * 1024
ENCODE_LIMIT = 60 * 1024 * 1024


def plan(widths, replicas):
    starts, at = [], 0
    for width in widths:
        count = width // LANES
        starts.append((at, at + count))
        at += 2 * count
    scales = tuple(at + slot for slot in range(3))
    per_home = -(-(at + 3) // replicas)
    return tuple(starts), scales, per_home


def exponent(peak):
    power = jnp.ceil(STEPS * jnp.log2(jnp.maximum(peak, 2.0**-120)))
    return jnp.clip(power, -120.0 * STEPS, 128.0 * STEPS - 1.0)


def encode_kernel(starts, scales, per_home, wg, wu, wd, gg, gu, gd, out, vwg, vwu, vwd, vgg, vgu, vgd, sems):
    rows = wg.shape[1]
    pairs = ((wd, vwd), (gd, vgd), (wg, vwg), (gg, vgg), (wu, vwu), (gu, vgu))
    copies = [pltpu.make_async_copy(src, dst, sems.at[i]) for i, (src, dst) in enumerate(pairs)]
    for copy in copies:
        copy.start()

    def put(tile, value):
        home, place = divmod(tile, per_home)
        out[home, place * rows : (place + 1) * rows, :] = value

    def coded(block_ref, first):
        count = block_ref.shape[2] // LANES
        peak = jnp.zeros((rows, LANES), jnp.float32)
        for c in range(count):
            peak = jnp.maximum(peak, jnp.abs(block_ref[0, :, c * LANES : (c + 1) * LANES].astype(jnp.float32)))
        power = exponent(jnp.max(peak, axis=(0, 1), keepdims=True))
        factor = jnp.broadcast_to(jnp.exp2(power * (-1.0 / STEPS)), (rows, LANES))
        for c in range(count):
            x = block_ref[0, :, c * LANES : (c + 1) * LANES].astype(jnp.float32)
            level = jnp.minimum(TOP * jnp.sqrt(jnp.abs(x) * factor), TOP) + 0.5
            level = jnp.where(x < 0, -level, level)
            put(first + c, level.astype(jnp.int32).astype(jnp.int16))
        return jnp.broadcast_to(power, (rows, LANES)).astype(jnp.int32)

    for tile in range(scales[2] + 1, out.shape[0] * per_home):
        put(tile, jnp.zeros((rows, LANES), jnp.int16))
    upper = lax.broadcasted_iota(jnp.int32, (rows, LANES), 0) < 8
    for at, (slot, w, g) in enumerate(((2, vwd, vgd), (0, vwg, vgg), (1, vwu, vgu))):
        copies[2 * at].wait()
        power_w = coded(w, starts[slot][0])
        copies[2 * at + 1].wait()
        power_g = coded(g, starts[slot][1])
        put(scales[slot], jnp.where(upper, power_w, power_g).astype(jnp.int16))


def swap_kernel(starts, scales, per_home, rows, partner, me, inp, out):
    replicas = inp.shape[0]
    for place in range(per_home):
        tile = me[0] * per_home + place
        slot = jnp.where(tile < starts[1][0], 0, jnp.where(tile < starts[2][0], 1, 2))
        slot = jnp.where(tile == scales[0], 0, jnp.where(tile == scales[1], 1, slot))
        for r in range(replicas):
            source = partner[slot, r]
            out[r, place * rows : (place + 1) * rows, :] = inp[source, place * rows : (place + 1) * rows, :]


def reader(per_home, rows, payload):
    def get(tile):
        home, place = divmod(tile, per_home)
        return payload[home, place * rows : (place + 1) * rows, :].astype(jnp.int32).astype(jnp.float32)

    return get


def decoded(code, scale):
    a = code * (1.0 / TOP)
    return a * jnp.abs(a) * scale


def scales_of(get, tile):
    power = jnp.exp2(get(tile) * (1.0 / STEPS))
    return power[0:1, :], power[8:9, :]


def squares_kernel(starts, scales, per_home, payload, gg, gu, gd, out):
    rows = gg.shape[1]
    get = reader(per_home, rows, payload)
    lane = lax.broadcasted_iota(jnp.int32, (1, LANES), 1)
    total = jnp.zeros((1, LANES), jnp.float32)
    for slot, g in enumerate((gg, gu, gd)):
        _, scale = scales_of(get, scales[slot])
        sums = jnp.zeros((rows, LANES), jnp.float32)
        for c in range(g.shape[2] // LANES):
            own = g[0, :, c * LANES : (c + 1) * LANES].astype(jnp.float32)
            mixed = 0.5 * (own + decoded(get(starts[slot][1] + c), scale))
            sums = sums + mixed * mixed
        total = jnp.where(lane == slot, jnp.sum(sums, axis=(0, 1), keepdims=True), total)
    out[...] = jnp.broadcast_to(total[None], out.shape)


def update_kernel(starts, scales, per_home, elements, sums, payload, wg, wu, wd, mg, mu, md, gg, gu, gd, og, ou, od, ng, nu, nd):
    rows = gg.shape[1]
    get = reader(per_home, rows, payload)
    lane = lax.broadcasted_iota(jnp.int32, (1, LANES), 1)
    totals = jnp.sum(sums[...], axis=0)
    groups = ((wg, mg, gg, og, ng), (wu, mu, gu, ou, nu), (wd, md, gd, od, nd))
    for slot, (w, m, g, o, n) in enumerate(groups):
        scale_w, scale_g = scales_of(get, scales[slot])
        squares = jnp.sum(jnp.where(lane == slot, totals, 0.0), axis=(0, 1), keepdims=True)
        bound = CLIP_RATIO * float(elements[slot]) ** 0.5
        clip = jnp.broadcast_to(jnp.minimum(1.0, bound / jnp.sqrt(squares + EPS)), (rows, LANES))
        for c in range(w.shape[2] // LANES):
            part = slice(c * LANES, (c + 1) * LANES)
            own = g[0, :, part].astype(jnp.float32)
            mixed = 0.5 * (own + decoded(get(starts[slot][1] + c), scale_g))
            mate = decoded(get(starts[slot][0] + c), scale_w)
            scaled = clip * mixed
            moment = BETA * m[0, :, part] + scaled
            weight = w[0, :, part]
            n[0, :, part] = moment
            o[0, :, part] = weight - GAMMA * (weight - mate) - RATE * (scaled + BETA * moment)


def local(partner, wg, wu, wd, mg, mu, md, gg, gu, gd):
    replicas = lax.axis_size("rep")
    shards = lax.axis_size("fsdp") * lax.axis_size("tp")
    rows = wg.shape[1]
    starts, scales, per_home = plan((wg.shape[2], wu.shape[2], wd.shape[2]), replicas)
    params = pltpu.CompilerParams(vmem_limit_bytes=VMEM_LIMIT)
    vmem = pl.BlockSpec(memory_space=pltpu.VMEM)
    smem = pl.BlockSpec(memory_space=pltpu.SMEM)
    packed = jax.ShapeDtypeStruct((replicas, per_home * rows, LANES), jnp.int16)

    coded = pl.pallas_call(
        functools.partial(encode_kernel, starts, scales, per_home),
        out_shape=packed,
        in_specs=[pl.BlockSpec(memory_space=pl.ANY)] * 6,
        out_specs=vmem,
        scratch_shapes=[pltpu.VMEM(a.shape, a.dtype) for a in (wg, wu, wd, gg, gu, gd)] + [pltpu.SemaphoreType.DMA((6,))],
        compiler_params=pltpu.CompilerParams(vmem_limit_bytes=ENCODE_LIMIT),
        name="encode",
    )(wg, wu, wd, gg, gu, gd)
    homed = lax.all_to_all(coded, "rep", 0, 0, tiled=True)
    me = lax.axis_index("rep").reshape(1).astype(jnp.int32)
    swapped = pl.pallas_call(
        functools.partial(swap_kernel, starts, scales, per_home, rows),
        out_shape=packed,
        in_specs=[smem, smem, vmem],
        out_specs=vmem,
        compiler_params=params,
        name="swap",
    )(partner, me, homed)
    mates = lax.all_to_all(swapped, "rep", 0, 0, tiled=True)
    partial = pl.pallas_call(
        functools.partial(squares_kernel, starts, scales, per_home),
        out_shape=jax.ShapeDtypeStruct((shards, 1, LANES), jnp.float32),
        in_specs=[vmem] * 4,
        out_specs=vmem,
        compiler_params=params,
        name="squares",
    )(mates, gg, gu, gd)
    sums = lax.all_to_all(partial, ("fsdp", "tp"), 0, 0, tiled=True)
    elements = tuple(shards * w.shape[1] * w.shape[2] for w in (wg, wu, wd))
    arrays = [jax.ShapeDtypeStruct(a.shape, jnp.float32) for a in (wg, wu, wd, mg, mu, md)]
    return pl.pallas_call(
        functools.partial(update_kernel, starts, scales, per_home, elements),
        out_shape=arrays,
        in_specs=[vmem] * 11,
        out_specs=[vmem] * 6,
        compiler_params=params,
        name="update",
    )(sums, mates, wg, wu, wd, mg, mu, md, gg, gu, gd)


def solution(mesh):
    spec = P("rep", "fsdp", "tp")
    return jax.shard_map(
        local,
        mesh=mesh,
        in_specs=(P(),) + (spec,) * 9,
        out_specs=(spec,) * 6,
        check_vma=False,
    )
```

```python
import functools

import jax
import jax.numpy as jnp
from jax import lax
from jax.experimental import pallas as pl
from jax.experimental.pallas import tpu as pltpu
from jax.sharding import PartitionSpec as P

CLIP_RATIO = 0.5
BETA = 0.9
GAMMA = 0.4
RATE = 0.7
EPS = 1e-06

LANES = 128
TOP = 32767.0
STEPS = 16.0
VMEM_LIMIT = 24 * 1024 * 1024
ENCODE_LIMIT = 60 * 1024 * 1024


def plan(widths, replicas):
    starts, at = [], 0
    for width in widths:
        count = width // LANES
        starts.append((at, at + count))
        at += 2 * count
    scales = tuple(at + slot for slot in range(3))
    per_home = -(-(at + 3) // replicas)
    return tuple(starts), scales, per_home


def locate(parts, cuts, place):
    for part, cut in zip(parts, cuts):
        if place < cut:
            return part, place
        place -= cut
    raise ValueError("place")


def exponent(peak):
    power = jnp.ceil(STEPS * jnp.log2(jnp.maximum(peak, 2.0**-120)))
    return jnp.clip(power, -120.0 * STEPS, 128.0 * STEPS - 1.0)


def encode_kernel(starts, scales, cuts, wg, wu, wd, gg, gu, gd, *refs):
    outs, (vwg, vwu, vwd, vgg, vgu, vgd, sems) = refs[: len(cuts)], refs[len(cuts) :]
    rows = wg.shape[1]
    per_home = sum(cuts)
    pairs = ((wd, vwd), (gd, vgd), (wg, vwg), (gg, vgg), (wu, vwu), (gu, vgu))
    copies = [pltpu.make_async_copy(src, dst, sems.at[i]) for i, (src, dst) in enumerate(pairs)]
    for copy in copies:
        copy.start()

    def put(tile, value):
        home, place = divmod(tile, per_home)
        out, place = locate(outs, cuts, place)
        out[home, place * rows : (place + 1) * rows, :] = value

    def coded(block_ref, first):
        count = block_ref.shape[2] // LANES
        peak = jnp.zeros((rows, LANES), jnp.float32)
        for c in range(count):
            peak = jnp.maximum(peak, jnp.abs(block_ref[0, :, c * LANES : (c + 1) * LANES].astype(jnp.float32)))
        power = exponent(jnp.max(peak, axis=(0, 1), keepdims=True))
        factor = jnp.broadcast_to(jnp.exp2(power * (-1.0 / STEPS)), (rows, LANES))
        for c in range(count):
            x = block_ref[0, :, c * LANES : (c + 1) * LANES].astype(jnp.float32)
            level = jnp.minimum(TOP * jnp.sqrt(jnp.abs(x) * factor), TOP) + 0.5
            level = jnp.where(x < 0, -level, level)
            put(first + c, level.astype(jnp.int32).astype(jnp.int16))
        return jnp.broadcast_to(power, (rows, LANES)).astype(jnp.int32)

    for tile in range(scales[2] + 1, outs[0].shape[0] * per_home):
        put(tile, jnp.zeros((rows, LANES), jnp.int16))
    upper = lax.broadcasted_iota(jnp.int32, (rows, LANES), 0) < 8
    for at, (slot, w, g) in enumerate(((2, vwd, vgd), (0, vwg, vgg), (1, vwu, vgu))):
        copies[2 * at].wait()
        power_w = coded(w, starts[slot][0])
        copies[2 * at + 1].wait()
        power_g = coded(g, starts[slot][1])
        put(scales[slot], jnp.where(upper, power_w, power_g).astype(jnp.int16))


def swap_kernel(starts, scales, cuts, rows, partner, me, *refs):
    inps, out = refs[:-1], refs[-1]
    replicas = out.shape[0]
    per_home = sum(cuts)
    for place in range(per_home):
        tile = me[0] * per_home + place
        slot = jnp.where(tile < starts[1][0], 0, jnp.where(tile < starts[2][0], 1, 2))
        slot = jnp.where(tile == scales[0], 0, jnp.where(tile == scales[1], 1, slot))
        inp, at = locate(inps, cuts, place)
        for r in range(replicas):
            source = partner[slot, r]
            out[r, place * rows : (place + 1) * rows, :] = inp[source, at * rows : (at + 1) * rows, :]


def reader(per_home, rows, payload):
    def get(tile):
        home, place = divmod(tile, per_home)
        return payload[home, place * rows : (place + 1) * rows, :].astype(jnp.int32).astype(jnp.float32)

    return get


def decoded(code, scale):
    a = code * (1.0 / TOP)
    return a * jnp.abs(a) * scale


def scales_of(get, tile):
    power = jnp.exp2(get(tile) * (1.0 / STEPS))
    return power[0:1, :], power[8:9, :]


def squares_kernel(starts, scales, per_home, payload, gg, gu, gd, out):
    rows = gg.shape[1]
    get = reader(per_home, rows, payload)
    lane = lax.broadcasted_iota(jnp.int32, (1, LANES), 1)
    total = jnp.zeros((1, LANES), jnp.float32)
    for slot, g in enumerate((gg, gu, gd)):
        _, scale = scales_of(get, scales[slot])
        sums = jnp.zeros((rows, LANES), jnp.float32)
        for c in range(g.shape[2] // LANES):
            own = g[0, :, c * LANES : (c + 1) * LANES].astype(jnp.float32)
            mixed = 0.5 * (own + decoded(get(starts[slot][1] + c), scale))
            sums = sums + mixed * mixed
        total = jnp.where(lane == slot, jnp.sum(sums, axis=(0, 1), keepdims=True), total)
    out[...] = jnp.broadcast_to(total[None], out.shape)


def update_kernel(starts, scales, per_home, elements, sums, payload, wg, wu, wd, mg, mu, md, gg, gu, gd, og, ou, od, ng, nu, nd):
    rows = gg.shape[1]
    get = reader(per_home, rows, payload)
    lane = lax.broadcasted_iota(jnp.int32, (1, LANES), 1)
    totals = jnp.sum(sums[...], axis=0)
    groups = ((wg, mg, gg, og, ng), (wu, mu, gu, ou, nu), (wd, md, gd, od, nd))
    for slot, (w, m, g, o, n) in enumerate(groups):
        scale_w, scale_g = scales_of(get, scales[slot])
        squares = jnp.sum(jnp.where(lane == slot, totals, 0.0), axis=(0, 1), keepdims=True)
        bound = CLIP_RATIO * float(elements[slot]) ** 0.5
        clip = jnp.broadcast_to(jnp.minimum(1.0, bound / jnp.sqrt(squares + EPS)), (rows, LANES))
        for c in range(w.shape[2] // LANES):
            part = slice(c * LANES, (c + 1) * LANES)
            own = g[0, :, part].astype(jnp.float32)
            mixed = 0.5 * (own + decoded(get(starts[slot][1] + c), scale_g))
            mate = decoded(get(starts[slot][0] + c), scale_w)
            scaled = clip * mixed
            moment = BETA * m[0, :, part] + scaled
            weight = w[0, :, part]
            n[0, :, part] = moment
            o[0, :, part] = weight - GAMMA * (weight - mate) - RATE * (scaled + BETA * moment)


def local(partner, wg, wu, wd, mg, mu, md, gg, gu, gd):
    replicas = lax.axis_size("rep")
    shards = lax.axis_size("fsdp") * lax.axis_size("tp")
    rows = wg.shape[1]
    starts, scales, per_home = plan((wg.shape[2], wu.shape[2], wd.shape[2]), replicas)
    params = pltpu.CompilerParams(vmem_limit_bytes=VMEM_LIMIT)
    vmem = pl.BlockSpec(memory_space=pltpu.VMEM)
    smem = pl.BlockSpec(memory_space=pltpu.SMEM)
    packed = jax.ShapeDtypeStruct((replicas, per_home * rows, LANES), jnp.int16)

    me = lax.axis_index("rep").reshape(1).astype(jnp.int32)

    def outward(cuts, *operands):
        coded = pl.pallas_call(
            functools.partial(encode_kernel, starts, scales, cuts),
            out_shape=[jax.ShapeDtypeStruct((replicas, cut * rows, LANES), jnp.int16) for cut in cuts],
            in_specs=[pl.BlockSpec(memory_space=pl.ANY)] * 6,
            out_specs=[vmem] * len(cuts),
            scratch_shapes=[pltpu.VMEM(a.shape, a.dtype) for a in operands[2:]] + [pltpu.SemaphoreType.DMA((6,))],
            compiler_params=pltpu.CompilerParams(vmem_limit_bytes=ENCODE_LIMIT),
            name="encode",
        )(*operands[2:])
        coded = list(coded)
        homed = []
        for i in range(len(cuts)):
            homed.append(lax.all_to_all(coded[i], "rep", 0, 0, tiled=True))
            if i + 1 < len(cuts):
                homed[i], coded[i + 1] = lax.optimization_barrier((homed[i], coded[i + 1]))
        return pl.pallas_call(
            functools.partial(swap_kernel, starts, scales, cuts, rows),
            out_shape=packed,
            in_specs=[smem, smem] + [vmem] * len(cuts),
            out_specs=vmem,
            compiler_params=params,
            name="swap",
        )(operands[0], operands[1], *homed)

    swapped = lax.cond(
        lax.rem(lax.axis_index("fsdp"), 2) == 1,
        functools.partial(outward, (1, per_home - 1)),
        functools.partial(outward, (per_home,)),
        partner, me, wg, wu, wd, gg, gu, gd,
    )
    mates = lax.all_to_all(swapped, "rep", 0, 0, tiled=True)
    partial = pl.pallas_call(
        functools.partial(squares_kernel, starts, scales, per_home),
        out_shape=jax.ShapeDtypeStruct((shards, 1, LANES), jnp.float32),
        in_specs=[vmem] * 4,
        out_specs=vmem,
        compiler_params=params,
        name="squares",
    )(mates, gg, gu, gd)
    sums = lax.all_to_all(partial, ("fsdp", "tp"), 0, 0, tiled=True)
    elements = tuple(shards * w.shape[1] * w.shape[2] for w in (wg, wu, wd))
    arrays = [jax.ShapeDtypeStruct(a.shape, jnp.float32) for a in (wg, wu, wd, mg, mu, md)]
    return pl.pallas_call(
        functools.partial(update_kernel, starts, scales, per_home, elements),
        out_shape=arrays,
        in_specs=[vmem] * 11,
        out_specs=[vmem] * 6,
        compiler_params=params,
        name="update",
    )(sums, mates, wg, wu, wd, mg, mu, md, gg, gu, gd)


def solution(mesh):
    spec = P("rep", "fsdp", "tp")
    return jax.shard_map(
        local,
        mesh=mesh,
        in_specs=(P(),) + (spec,) * 9,
        out_specs=(spec,) * 6,
        check_vma=False,
    )
```

```python
import functools

import jax
import jax.numpy as jnp
from jax import lax
from jax.experimental import pallas as pl
from jax.experimental.pallas import tpu as pltpu
from jax.sharding import PartitionSpec as P

CLIP_RATIO = 0.5
BETA = 0.9
GAMMA = 0.4
RATE = 0.7
EPS = 1e-06

LANES = 128
TOP = 32767.0
STEPS = 16.0
TINY = 2.0**-120
VMEM_LIMIT = 24 * 1024 * 1024
ENCODE_LIMIT = 60 * 1024 * 1024


def plan(widths, replicas):
    starts, at = [], 0
    for width in widths:
        count = width // LANES
        starts.append((at, at + count))
        at += 2 * count
    scales = tuple(at + slot for slot in range(3))
    per_home = -(-(at + 3) // replicas)
    return tuple(starts), scales, per_home


def locate(parts, cuts, place):
    for part, cut in zip(parts, cuts):
        if place < cut:
            return part, place
        place -= cut
    raise ValueError("place")


def exponent(peak):
    power = jnp.ceil(STEPS * jnp.log2(jnp.maximum(peak, TINY)))
    return jnp.clip(power, -120.0 * STEPS, 128.0 * STEPS - 1.0)


def encode_kernel(starts, scales, cuts, wg, wu, wd, gg, gu, gd, *refs):
    outs, (vwg, vwu, vwd, vgg, vgu, vgd, sems) = refs[: len(cuts)], refs[len(cuts) :]
    rows = wg.shape[1]
    per_home = sum(cuts)
    pairs = ((wd, vwd), (gd, vgd), (wg, vwg), (gg, vgg), (wu, vwu), (gu, vgu))
    copies = [pltpu.make_async_copy(src, dst, sems.at[i]) for i, (src, dst) in enumerate(pairs)]
    for copy in copies:
        copy.start()

    def put(tile, value):
        home, place = divmod(tile, per_home)
        out, place = locate(outs, cuts, place)
        out[home, place * rows : (place + 1) * rows, :] = value

    def coded(block_ref, first):
        count = block_ref.shape[2] // LANES
        peak = jnp.abs(block_ref[0, :, 0:LANES])
        for c in range(1, count):
            peak = jnp.maximum(peak, jnp.abs(block_ref[0, :, c * LANES : (c + 1) * LANES]))
        power = exponent(jnp.max(peak.astype(jnp.float32), axis=(0, 1), keepdims=True))
        factor = jnp.broadcast_to(TOP * jnp.exp2(power * (-0.5 / STEPS)), (rows, LANES))
        for c in range(count):
            x = block_ref[0, :, c * LANES : (c + 1) * LANES].astype(jnp.float32)
            level = x * lax.rsqrt(jnp.maximum(jnp.abs(x), TINY)) * factor
            level = jnp.clip(level, -TOP, TOP) + jnp.where(x < 0, -0.5, 0.5)
            put(first + c, level.astype(jnp.int32).astype(jnp.int16))
        return jnp.broadcast_to(power, (rows, LANES)).astype(jnp.int32)

    for tile in range(scales[2] + 1, outs[0].shape[0] * per_home):
        put(tile, jnp.zeros((rows, LANES), jnp.int16))
    upper = lax.broadcasted_iota(jnp.int32, (rows, LANES), 0) < 8
    for at, (slot, w, g) in enumerate(((2, vwd, vgd), (0, vwg, vgg), (1, vwu, vgu))):
        copies[2 * at].wait()
        power_w = coded(w, starts[slot][0])
        copies[2 * at + 1].wait()
        power_g = coded(g, starts[slot][1])
        put(scales[slot], jnp.where(upper, power_w, power_g).astype(jnp.int16))


def swap_kernel(starts, scales, cuts, rows, partner_hbm, me, *refs):
    inps, (out, partner, sem) = refs[: len(cuts)], refs[len(cuts) :]
    fetch = pltpu.make_async_copy(partner_hbm, partner, sem)
    fetch.start()
    fetch.wait()
    replicas = out.shape[0]
    per_home = sum(cuts)
    for place in range(per_home):
        tile = me[0] * per_home + place
        slot = jnp.where(tile < starts[1][0], 0, jnp.where(tile < starts[2][0], 1, 2))
        slot = jnp.where(tile == scales[0], 0, jnp.where(tile == scales[1], 1, slot))
        inp, at = locate(inps, cuts, place)
        for r in range(replicas):
            source = partner[slot, r]
            out[r, place * rows : (place + 1) * rows, :] = inp[source, at * rows : (at + 1) * rows, :]


def reader(per_home, rows, payload):
    def get(tile):
        home, place = divmod(tile, per_home)
        return payload[home, place * rows : (place + 1) * rows, :].astype(jnp.int32).astype(jnp.float32)

    return get


def decoded(code, scale):
    a = code * (1.0 / TOP)
    return a * jnp.abs(a) * scale


def scales_of(get, tile):
    power = jnp.exp2(get(tile) * (1.0 / STEPS))
    return power[0:1, :], power[8:9, :]


def squares_kernel(starts, scales, per_home, payload, gg, gu, gd, out):
    rows = gg.shape[1]
    get = reader(per_home, rows, payload)
    lane = lax.broadcasted_iota(jnp.int32, (1, LANES), 1)
    total = jnp.zeros((1, LANES), jnp.float32)
    for slot, g in enumerate((gg, gu, gd)):
        _, scale = scales_of(get, scales[slot])
        sums = jnp.zeros((rows, LANES), jnp.float32)
        for c in range(g.shape[2] // LANES):
            own = g[0, :, c * LANES : (c + 1) * LANES].astype(jnp.float32)
            mixed = 0.5 * (own + decoded(get(starts[slot][1] + c), scale))
            sums = sums + mixed * mixed
        total = jnp.where(lane == slot, jnp.sum(sums, axis=(0, 1), keepdims=True), total)
    out[...] = jnp.broadcast_to(total[None], out.shape)


def update_kernel(starts, scales, per_home, elements, sums, payload, wg, wu, wd, mg, mu, md, gg, gu, gd, *refs):
    outs, (og, ou, od, ng, nu, nd), sems = refs[:6], refs[6:12], refs[12]
    copies = [pltpu.make_async_copy(src, dst, sems.at[i]) for i, (src, dst) in enumerate(zip(refs[6:12], outs))]
    rows = gg.shape[1]
    get = reader(per_home, rows, payload)
    lane = lax.broadcasted_iota(jnp.int32, (1, LANES), 1)
    totals = jnp.sum(sums[...], axis=0)
    groups = ((wg, mg, gg, og, ng), (wu, mu, gu, ou, nu), (wd, md, gd, od, nd))
    for slot, (w, m, g, o, n) in enumerate(groups):
        scale_w, scale_g = scales_of(get, scales[slot])
        squares = jnp.sum(jnp.where(lane == slot, totals, 0.0), axis=(0, 1), keepdims=True)
        bound = CLIP_RATIO * float(elements[slot]) ** 0.5
        clip = jnp.broadcast_to(jnp.minimum(1.0, bound / jnp.sqrt(squares + EPS)), (rows, LANES))
        for c in range(w.shape[2] // LANES):
            part = slice(c * LANES, (c + 1) * LANES)
            own = g[0, :, part].astype(jnp.float32)
            mixed = 0.5 * (own + decoded(get(starts[slot][1] + c), scale_g))
            mate = decoded(get(starts[slot][0] + c), scale_w)
            scaled = clip * mixed
            moment = BETA * m[0, :, part] + scaled
            weight = w[0, :, part]
            n[0, :, part] = moment
            o[0, :, part] = weight - GAMMA * (weight - mate) - RATE * (scaled + BETA * moment)
        copies[slot].start()
        copies[3 + slot].start()
    for copy in copies:
        copy.wait()


def local(partner, wg, wu, wd, mg, mu, md, gg, gu, gd):
    replicas = lax.axis_size("rep")
    shards = lax.axis_size("fsdp") * lax.axis_size("tp")
    rows = wg.shape[1]
    starts, scales, per_home = plan((wg.shape[2], wu.shape[2], wd.shape[2]), replicas)
    params = pltpu.CompilerParams(vmem_limit_bytes=VMEM_LIMIT)
    vmem = pl.BlockSpec(memory_space=pltpu.VMEM)
    smem = pl.BlockSpec(memory_space=pltpu.SMEM)
    packed = jax.ShapeDtypeStruct((replicas, per_home * rows, LANES), jnp.int16)

    me = lax.axis_index("rep").reshape(1).astype(jnp.int32)

    def outward(cuts, *operands):
        coded = pl.pallas_call(
            functools.partial(encode_kernel, starts, scales, cuts),
            out_shape=[jax.ShapeDtypeStruct((replicas, cut * rows, LANES), jnp.int16) for cut in cuts],
            in_specs=[pl.BlockSpec(memory_space=pl.ANY)] * 6,
            out_specs=[vmem] * len(cuts),
            scratch_shapes=[pltpu.VMEM(a.shape, a.dtype) for a in operands[2:]] + [pltpu.SemaphoreType.DMA((6,))],
            compiler_params=pltpu.CompilerParams(vmem_limit_bytes=ENCODE_LIMIT),
            name="encode",
        )(*operands[2:])
        coded = list(coded)
        homed = []
        for i in range(len(cuts)):
            homed.append(lax.all_to_all(coded[i], "rep", 0, 0, tiled=True))
            if i + 1 < len(cuts):
                homed[i], coded[i + 1] = lax.optimization_barrier((homed[i], coded[i + 1]))
        return pl.pallas_call(
            functools.partial(swap_kernel, starts, scales, cuts, rows),
            out_shape=packed,
            in_specs=[pl.BlockSpec(memory_space=pl.ANY), smem] + [vmem] * len(cuts),
            out_specs=vmem,
            scratch_shapes=[pltpu.SMEM(partner.shape, partner.dtype), pltpu.SemaphoreType.DMA],
            compiler_params=params,
            name="swap",
        )(operands[0], operands[1], *homed)

    z_lo, core = jnp.divmod(lax.axis_index("fsdp"), 2)
    inner = (z_lo == 1) | (z_lo == 2)
    swapped = lax.cond(
        inner == (core == 0),
        functools.partial(outward, (1, per_home - 1)),
        functools.partial(outward, (per_home,)),
        partner, me, wg, wu, wd, gg, gu, gd,
    )
    mates = lax.all_to_all(swapped, "rep", 0, 0, tiled=True)
    partial = pl.pallas_call(
        functools.partial(squares_kernel, starts, scales, per_home),
        out_shape=jax.ShapeDtypeStruct((shards, 1, LANES), jnp.float32),
        in_specs=[vmem] * 4,
        out_specs=vmem,
        compiler_params=params,
        name="squares",
    )(mates, gg, gu, gd)
    sums = lax.all_to_all(partial, ("fsdp", "tp"), 0, 0, tiled=True)
    elements = tuple(shards * w.shape[1] * w.shape[2] for w in (wg, wu, wd))
    arrays = [jax.ShapeDtypeStruct(a.shape, jnp.float32) for a in (wg, wu, wd, mg, mu, md)]
    return pl.pallas_call(
        functools.partial(update_kernel, starts, scales, per_home, elements),
        out_shape=arrays,
        in_specs=[vmem] * 11,
        out_specs=[pl.BlockSpec(memory_space=pl.ANY)] * 6,
        scratch_shapes=[pltpu.VMEM(a.shape, a.dtype) for a in arrays] + [pltpu.SemaphoreType.DMA((6,))],
        compiler_params=params,
        name="update",
    )(sums, mates, wg, wu, wd, mg, mu, md, gg, gu, gd)


def solution(mesh):
    spec = P("rep", "fsdp", "tp")
    return jax.shard_map(
        local,
        mesh=mesh,
        in_specs=(P(),) + (spec,) * 9,
        out_specs=(spec,) * 6,
        check_vma=False,
    )
```

```python
import functools

import jax
import jax.numpy as jnp
from jax import lax
from jax.experimental import pallas as pl
from jax.experimental.pallas import tpu as pltpu
from jax.sharding import PartitionSpec as P

CLIP_RATIO = 0.5
BETA = 0.9
GAMMA = 0.4
RATE = 0.7
EPS = 1e-06

LANES = 128
TOP = 32767.0
STEPS = 16.0
TINY = 2.0**-120
VMEM_LIMIT = 24 * 1024 * 1024
ENCODE_LIMIT = 60 * 1024 * 1024


def plan(widths, replicas):
    counts = [width // LANES for width in widths]
    last = [(2, kind, c) for kind in range(2) for c in range(counts[2])]
    rest = [(slot, kind, c) for slot in range(2) for kind in range(2) for c in range(counts[slot])]
    rest += last[replicas:]
    bounds = (2 * counts[0], 2 * counts[0] + 2 * counts[1], len(rest))
    rest += [(slot, 2, 0) for slot in range(3)]
    more = -(-len(rest) // replicas)
    where = {tile: (i, 0) for i, tile in enumerate(last[:replicas])}
    where.update({tile: (i // more, 1 + i % more) for i, tile in enumerate(rest)})
    spare = [(i // more, 1 + i % more) for i in range(len(rest), more * replicas)]
    return where, spare, bounds, 1 + more


def exponent(peak):
    power = jnp.ceil(STEPS * jnp.log2(jnp.maximum(peak, TINY)))
    return jnp.clip(power, -120.0 * STEPS, 128.0 * STEPS - 1.0)


def encode_kernel(where, spare, first, count, names, *refs):
    n = len(names)
    srcs, out, dsts, sems = refs[:n], refs[n], refs[n + 1 : 2 * n + 1], refs[2 * n + 1]
    rows = srcs[0].shape[1]
    copies = [pltpu.make_async_copy(srcs[i], dsts[i], sems.at[i]) for i in range(n)]
    for copy in copies:
        copy.start()

    def put(at, value):
        home, place = at
        if first <= place < first + count:
            out[home, (place - first) * rows : (place - first + 1) * rows, :] = value

    for at in spare:
        put(at, jnp.zeros((rows, LANES), jnp.int16))
    powers = {}
    for (slot, kind), ref, copy in zip(names, dsts, copies):
        copy.wait()
        tiles = ref.shape[2] // LANES
        peak = jnp.abs(ref[0, :, 0:LANES])
        for c in range(1, tiles):
            peak = jnp.maximum(peak, jnp.abs(ref[0, :, c * LANES : (c + 1) * LANES]))
        power = exponent(jnp.max(peak.astype(jnp.float32), axis=(0, 1), keepdims=True))
        factor = jnp.broadcast_to(TOP * jnp.exp2(power * (-0.5 / STEPS)), (rows, LANES))
        for c in range(tiles):
            at = where[slot, kind, c]
            if first <= at[1] < first + count:
                x = ref[0, :, c * LANES : (c + 1) * LANES].astype(jnp.float32)
                level = x * lax.rsqrt(jnp.maximum(jnp.abs(x), TINY)) * factor
                level = jnp.round(jnp.clip(level, -TOP, TOP))
                put(at, level.astype(jnp.int32).astype(jnp.int16))
        powers[slot, kind] = jnp.broadcast_to(power, (rows, LANES)).astype(jnp.int32)
    if first + count > 1:
        upper = lax.broadcasted_iota(jnp.int32, (rows, LANES), 0) < 8
        for slot in range(3):
            put(where[slot, 2, 0], jnp.where(upper, powers[slot, 0], powers[slot, 1]).astype(jnp.int16))


def swap_kernel(bounds, cuts, rows, partner_hbm, me, *refs):
    inps, (out, partner, sem) = refs[: len(cuts)], refs[len(cuts) :]
    fetch = pltpu.make_async_copy(partner_hbm, partner, sem)
    fetch.start()
    fetch.wait()
    replicas = out.shape[0]
    more = sum(cuts) - 1
    for place in range(1 + more):
        slot = 2
        if place:
            tile = me[0] * more + place - 1
            slot = jnp.where(tile < bounds[0], 0, jnp.where(tile < bounds[1], 1, 2))
            slot = jnp.where(tile == bounds[2], 0, jnp.where(tile == bounds[2] + 1, 1, slot))
        inp, at = locate(inps, cuts, place)
        for r in range(replicas):
            source = partner[slot, r]
            out[r, place * rows : (place + 1) * rows, :] = inp[source, at * rows : (at + 1) * rows, :]


def locate(parts, cuts, place):
    for part, cut in zip(parts, cuts):
        if place < cut:
            return part, place
        place -= cut
    raise ValueError("place")


def reader(where, rows, payload):
    def get(*tile):
        home, place = where[tile]
        return payload[home, place * rows : (place + 1) * rows, :].astype(jnp.int32).astype(jnp.float32)

    return get


def decoded(code, scale):
    a = code * (1.0 / TOP)
    return a * jnp.abs(a) * scale


def scales_of(get, slot):
    power = jnp.exp2(get(slot, 2, 0) * (1.0 / STEPS))
    return power[0:1, :], power[8:9, :]


def squares_kernel(where, payload, gg, gu, gd, out):
    rows = gg.shape[1]
    get = reader(where, rows, payload)
    lane = lax.broadcasted_iota(jnp.int32, (1, LANES), 1)
    total = jnp.zeros((1, LANES), jnp.float32)
    for slot, g in enumerate((gg, gu, gd)):
        _, scale = scales_of(get, slot)
        sums = jnp.zeros((rows, LANES), jnp.float32)
        for c in range(g.shape[2] // LANES):
            own = g[0, :, c * LANES : (c + 1) * LANES].astype(jnp.float32)
            mixed = 0.5 * (own + decoded(get(slot, 1, c), scale))
            sums = sums + mixed * mixed
        total = jnp.where(lane == slot, jnp.sum(sums, axis=(0, 1), keepdims=True), total)
    out[...] = jnp.broadcast_to(total[None], out.shape)


def update_kernel(where, elements, sums, payload, wg, wu, wd, mg, mu, md, gg, gu, gd, *refs):
    outs, (og, ou, od, ng, nu, nd), sems = refs[:6], refs[6:12], refs[12]
    copies = [pltpu.make_async_copy(src, dst, sems.at[i]) for i, (src, dst) in enumerate(zip(refs[6:12], outs))]
    rows = gg.shape[1]
    get = reader(where, rows, payload)
    lane = lax.broadcasted_iota(jnp.int32, (1, LANES), 1)
    totals = jnp.sum(sums[...], axis=0)
    groups = ((wg, mg, gg, og, ng), (wu, mu, gu, ou, nu), (wd, md, gd, od, nd))
    for slot, (w, m, g, o, n) in enumerate(groups):
        scale_w, scale_g = scales_of(get, slot)
        squares = jnp.sum(jnp.where(lane == slot, totals, 0.0), axis=(0, 1), keepdims=True)
        bound = CLIP_RATIO * float(elements[slot]) ** 0.5
        clip = jnp.broadcast_to(jnp.minimum(1.0, bound / jnp.sqrt(squares + EPS)), (rows, LANES))
        for c in range(w.shape[2] // LANES):
            part = slice(c * LANES, (c + 1) * LANES)
            own = g[0, :, part].astype(jnp.float32)
            mixed = 0.5 * (own + decoded(get(slot, 1, c), scale_g))
            mate = decoded(get(slot, 0, c), scale_w)
            scaled = clip * mixed
            moment = BETA * m[0, :, part] + scaled
            weight = w[0, :, part]
            n[0, :, part] = moment
            o[0, :, part] = weight - GAMMA * (weight - mate) - RATE * (scaled + BETA * moment)
        copies[slot].start()
        copies[3 + slot].start()
    for copy in copies:
        copy.wait()


def local(partner, wg, wu, wd, mg, mu, md, gg, gu, gd):
    replicas = lax.axis_size("rep")
    shards = lax.axis_size("fsdp") * lax.axis_size("tp")
    rows = wg.shape[1]
    where, spare, bounds, per_home = plan((wg.shape[2], wu.shape[2], wd.shape[2]), replicas)
    params = pltpu.CompilerParams(vmem_limit_bytes=VMEM_LIMIT)
    vmem = pl.BlockSpec(memory_space=pltpu.VMEM)
    smem = pl.BlockSpec(memory_space=pltpu.SMEM)
    packed = jax.ShapeDtypeStruct((replicas, per_home * rows, LANES), jnp.int16)

    me = lax.axis_index("rep").reshape(1).astype(jnp.int32)

    def encode(arrays, first, count):
        return pl.pallas_call(
            functools.partial(encode_kernel, where, spare, first, count, tuple(arrays)),
            out_shape=jax.ShapeDtypeStruct((replicas, count * rows, LANES), jnp.int16),
            in_specs=[pl.BlockSpec(memory_space=pl.ANY)] * len(arrays),
            out_specs=vmem,
            scratch_shapes=[pltpu.VMEM(a.shape, a.dtype) for a in arrays.values()]
            + [pltpu.SemaphoreType.DMA((len(arrays),))],
            compiler_params=pltpu.CompilerParams(vmem_limit_bytes=ENCODE_LIMIT),
            name="encode",
        )(*arrays.values())

    def swap(partner, me, cuts, homed):
        return pl.pallas_call(
            functools.partial(swap_kernel, bounds, cuts, rows),
            out_shape=packed,
            in_specs=[pl.BlockSpec(memory_space=pl.ANY), smem] + [vmem] * len(cuts),
            out_specs=vmem,
            scratch_shapes=[pltpu.SMEM(partner.shape, partner.dtype), pltpu.SemaphoreType.DMA],
            compiler_params=params,
            name="swap",
        )(partner, me, *homed)

    def named(wg, wu, wd, gg, gu, gd):
        return {(2, 0): wd, (2, 1): gd, (0, 0): wg, (0, 1): gg, (1, 0): wu, (1, 1): gu}

    def early(partner, me, *arrays):
        coded = encode(named(*arrays), 0, per_home)
        return swap(partner, me, (per_home,), (lax.all_to_all(coded, "rep", 0, 0, tiled=True),))

    def late(partner, me, *arrays):
        named_arrays = named(*arrays)
        down = {key: a for key, a in named_arrays.items() if key[0] == 2}
        head = lax.all_to_all(encode(down, 0, 1), "rep", 0, 0, tiled=True)
        coded = encode(named_arrays, 1, per_home - 1)
        head, coded = lax.optimization_barrier((head, coded))
        tail = lax.all_to_all(coded, "rep", 0, 0, tiled=True)
        return swap(partner, me, (1, per_home - 1), (head, tail))

    z_lo, core = jnp.divmod(lax.axis_index("fsdp"), 2)
    swapped = lax.cond(
        lax.rem(z_lo + core, 2) == 0,
        late,
        early,
        partner, me, wg, wu, wd, gg, gu, gd,
    )
    mates = lax.all_to_all(swapped, "rep", 0, 0, tiled=True)
    partial = pl.pallas_call(
        functools.partial(squares_kernel, where),
        out_shape=jax.ShapeDtypeStruct((shards, 1, LANES), jnp.float32),
        in_specs=[vmem] * 4,
        out_specs=vmem,
        compiler_params=params,
        name="squares",
    )(mates, gg, gu, gd)
    sums = lax.all_to_all(partial, ("fsdp", "tp"), 0, 0, tiled=True)
    elements = tuple(shards * w.shape[1] * w.shape[2] for w in (wg, wu, wd))
    arrays = [jax.ShapeDtypeStruct(a.shape, jnp.float32) for a in (wg, wu, wd, mg, mu, md)]
    return pl.pallas_call(
        functools.partial(update_kernel, where, elements),
        out_shape=arrays,
        in_specs=[vmem] * 11,
        out_specs=[pl.BlockSpec(memory_space=pl.ANY)] * 6,
        scratch_shapes=[pltpu.VMEM(a.shape, a.dtype) for a in arrays] + [pltpu.SemaphoreType.DMA((6,))],
        compiler_params=params,
        name="update",
    )(sums, mates, wg, wu, wd, mg, mu, md, gg, gu, gd)


def solution(mesh):
    spec = P("rep", "fsdp", "tp")
    return jax.shard_map(
        local,
        mesh=mesh,
        in_specs=(P(),) + (spec,) * 9,
        out_specs=(spec,) * 6,
        check_vma=False,
    )
```

```python
import functools

import jax
import jax.numpy as jnp
from jax import lax
from jax.experimental import pallas as pl
from jax.experimental.pallas import tpu as pltpu
from jax.sharding import PartitionSpec as P

CLIP_RATIO = 0.5
BETA = 0.9
GAMMA = 0.4
RATE = 0.7
EPS = 1e-06

LANES = 128
TOP = 32767.0
STEPS = 16.0
TINY = 2.0**-120
REPLICAS = 16
ORDER = 11
VMEM_LIMIT = 24 * 1024 * 1024
ENCODE_LIMIT = 60 * 1024 * 1024


def plan(widths, replicas):
    counts = [width // LANES for width in widths]
    last = [(2, kind, c) for kind in range(2) for c in range(counts[2])]
    rest = [(slot, kind, c) for slot in range(2) for kind in range(2) for c in range(counts[slot])]
    rest += last[replicas:]
    bounds = (2 * counts[0], 2 * counts[0] + 2 * counts[1], len(rest))
    rest += [(slot, 2, 0) for slot in range(3)]
    more = -(-len(rest) // replicas)
    where = {tile: (i, 0) for i, tile in enumerate(last[:replicas])}
    where.update({tile: (i // more, 1 + i % more) for i, tile in enumerate(rest)})
    spare = [(i // more, 1 + i % more) for i in range(len(rest), more * replicas)]
    return where, spare, bounds, 1 + more


def place_of(order, index):
    return (order + REPLICAS - index) % REPLICAS


def groups_of(order):
    return [[place_of(order, i) for i in range(REPLICAS)]]


def exponent(peak):
    power = jnp.ceil(STEPS * jnp.log2(jnp.maximum(peak, TINY)))
    return jnp.clip(power, -120.0 * STEPS, 128.0 * STEPS - 1.0)


def encode_kernel(where, spare, first, count, order, names, *refs):
    n = len(names)
    srcs, out, dsts, sems = refs[:n], refs[n], refs[n + 1 : 2 * n + 1], refs[2 * n + 1]
    rows = srcs[0].shape[1]
    copies = [pltpu.make_async_copy(srcs[i], dsts[i], sems.at[i]) for i in range(n)]
    for copy in copies:
        copy.start()

    def put(at, value):
        home, place = at
        if first <= place < first + count:
            out[place_of(order, home), (place - first) * rows : (place - first + 1) * rows, :] = value

    for at in spare:
        put(at, jnp.zeros((rows, LANES), jnp.int16))
    powers = {}
    for (slot, kind), ref, copy in zip(names, dsts, copies):
        copy.wait()
        tiles = ref.shape[2] // LANES
        peak = jnp.abs(ref[0, :, 0:LANES])
        for c in range(1, tiles):
            peak = jnp.maximum(peak, jnp.abs(ref[0, :, c * LANES : (c + 1) * LANES]))
        power = exponent(jnp.max(peak.astype(jnp.float32), axis=(0, 1), keepdims=True))
        factor = jnp.broadcast_to(TOP * jnp.exp2(power * (-0.5 / STEPS)), (rows, LANES))
        for c in range(tiles):
            at = where[slot, kind, c]
            if first <= at[1] < first + count:
                x = ref[0, :, c * LANES : (c + 1) * LANES].astype(jnp.float32)
                level = x * lax.rsqrt(jnp.maximum(jnp.abs(x), TINY)) * factor
                level = jnp.round(jnp.clip(level, -TOP, TOP))
                put(at, level.astype(jnp.int32).astype(jnp.int16))
        powers[slot, kind] = jnp.broadcast_to(power, (rows, LANES)).astype(jnp.int32)
    if first + count > 1:
        upper = lax.broadcasted_iota(jnp.int32, (rows, LANES), 0) < 8
        for slot in range(3):
            put(where[slot, 2, 0], jnp.where(upper, powers[slot, 0], powers[slot, 1]).astype(jnp.int16))


def swap_kernel(bounds, cuts, rows, order, partner_hbm, me, *refs):
    inps, (out, partner, sem) = refs[: len(cuts)], refs[len(cuts) :]
    fetch = pltpu.make_async_copy(partner_hbm, partner, sem)
    fetch.start()
    fetch.wait()
    replicas = out.shape[0]
    more = sum(cuts) - 1
    for place in range(1 + more):
        slot = 2
        if place:
            tile = me[0] * more + place - 1
            slot = jnp.where(tile < bounds[0], 0, jnp.where(tile < bounds[1], 1, 2))
            slot = jnp.where(tile == bounds[2], 0, jnp.where(tile == bounds[2] + 1, 1, slot))
        inp, at = locate(inps, cuts, place)
        for r in range(replicas):
            source = place_of(order, partner[slot, r])
            out[place_of(ORDER, r), place * rows : (place + 1) * rows, :] = inp[source, at * rows : (at + 1) * rows, :]


def locate(parts, cuts, place):
    for part, cut in zip(parts, cuts):
        if place < cut:
            return part, place
        place -= cut
    raise ValueError("place")


def reader(where, rows, payload):
    def get(*tile):
        home, place = where[tile]
        return payload[place_of(ORDER, home), place * rows : (place + 1) * rows, :].astype(jnp.int32).astype(jnp.float32)

    return get


def decoded(code, scale):
    a = code * (1.0 / TOP)
    return a * jnp.abs(a) * scale


def scales_of(get, slot):
    power = jnp.exp2(get(slot, 2, 0) * (1.0 / STEPS))
    return power[0:1, :], power[8:9, :]


def squares_kernel(where, payload, gg, gu, gd, out):
    rows = gg.shape[1]
    get = reader(where, rows, payload)
    lane = lax.broadcasted_iota(jnp.int32, (1, LANES), 1)
    total = jnp.zeros((1, LANES), jnp.float32)
    for slot, g in enumerate((gg, gu, gd)):
        _, scale = scales_of(get, slot)
        sums = jnp.zeros((rows, LANES), jnp.float32)
        for c in range(g.shape[2] // LANES):
            own = g[0, :, c * LANES : (c + 1) * LANES].astype(jnp.float32)
            mixed = 0.5 * (own + decoded(get(slot, 1, c), scale))
            sums = sums + mixed * mixed
        total = jnp.where(lane == slot, jnp.sum(sums, axis=(0, 1), keepdims=True), total)
    out[...] = jnp.broadcast_to(total[None], out.shape)


def update_kernel(where, elements, sums, payload, wg, wu, wd, mg, mu, md, gg, gu, gd, *refs):
    outs, (og, ou, od, ng, nu, nd), sems = refs[:6], refs[6:12], refs[12]
    copies = [pltpu.make_async_copy(src, dst, sems.at[i]) for i, (src, dst) in enumerate(zip(refs[6:12], outs))]
    rows = gg.shape[1]
    get = reader(where, rows, payload)
    lane = lax.broadcasted_iota(jnp.int32, (1, LANES), 1)
    totals = jnp.sum(sums[...], axis=0)
    groups = ((wg, mg, gg, og, ng), (wu, mu, gu, ou, nu), (wd, md, gd, od, nd))
    for slot, (w, m, g, o, n) in enumerate(groups):
        scale_w, scale_g = scales_of(get, slot)
        squares = jnp.sum(jnp.where(lane == slot, totals, 0.0), axis=(0, 1), keepdims=True)
        bound = CLIP_RATIO * float(elements[slot]) ** 0.5
        clip = jnp.broadcast_to(jnp.minimum(1.0, bound / jnp.sqrt(squares + EPS)), (rows, LANES))
        for c in range(w.shape[2] // LANES):
            part = slice(c * LANES, (c + 1) * LANES)
            own = g[0, :, part].astype(jnp.float32)
            mixed = 0.5 * (own + decoded(get(slot, 1, c), scale_g))
            mate = decoded(get(slot, 0, c), scale_w)
            scaled = clip * mixed
            moment = BETA * m[0, :, part] + scaled
            weight = w[0, :, part]
            n[0, :, part] = moment
            o[0, :, part] = weight - GAMMA * (weight - mate) - RATE * (scaled + BETA * moment)
        copies[slot].start()
        copies[3 + slot].start()
    for copy in copies:
        copy.wait()


def local(partner, wg, wu, wd, mg, mu, md, gg, gu, gd):
    replicas = lax.axis_size("rep")
    shards = lax.axis_size("fsdp") * lax.axis_size("tp")
    rows = wg.shape[1]
    where, spare, bounds, per_home = plan((wg.shape[2], wu.shape[2], wd.shape[2]), replicas)
    params = pltpu.CompilerParams(vmem_limit_bytes=VMEM_LIMIT)
    vmem = pl.BlockSpec(memory_space=pltpu.VMEM)
    smem = pl.BlockSpec(memory_space=pltpu.SMEM)
    packed = jax.ShapeDtypeStruct((replicas, per_home * rows, LANES), jnp.int16)

    me = lax.axis_index("rep").reshape(1).astype(jnp.int32)

    def encode(arrays, first, count, order):
        return pl.pallas_call(
            functools.partial(encode_kernel, where, spare, first, count, order, tuple(arrays)),
            out_shape=jax.ShapeDtypeStruct((replicas, count * rows, LANES), jnp.int16),
            in_specs=[pl.BlockSpec(memory_space=pl.ANY)] * len(arrays),
            out_specs=vmem,
            scratch_shapes=[pltpu.VMEM(a.shape, a.dtype) for a in arrays.values()]
            + [pltpu.SemaphoreType.DMA((len(arrays),))],
            compiler_params=pltpu.CompilerParams(vmem_limit_bytes=ENCODE_LIMIT),
            name="encode",
        )(*arrays.values())

    def swap(partner, me, cuts, order, homed):
        return pl.pallas_call(
            functools.partial(swap_kernel, bounds, cuts, rows, order),
            out_shape=packed,
            in_specs=[pl.BlockSpec(memory_space=pl.ANY), smem] + [vmem] * len(cuts),
            out_specs=vmem,
            scratch_shapes=[pltpu.SMEM(partner.shape, partner.dtype), pltpu.SemaphoreType.DMA],
            compiler_params=params,
            name="swap",
        )(partner, me, *homed)

    def named(wg, wu, wd, gg, gu, gd):
        return {(2, 0): wd, (2, 1): gd, (0, 0): wg, (0, 1): gg, (1, 0): wu, (1, 1): gu}

    def send(payload, order):
        return lax.all_to_all(payload, "rep", 0, 0, tiled=True, axis_index_groups=groups_of(order))

    def early(partner, me, *arrays):
        coded = encode(named(*arrays), 0, per_home, ORDER)
        return swap(partner, me, (per_home,), ORDER, (send(coded, ORDER),))

    def late(partner, me, *arrays):
        named_arrays = named(*arrays)
        down = {key: a for key, a in named_arrays.items() if key[0] == 2}
        head = send(encode(down, 0, 1, ORDER), ORDER)
        coded = encode(named_arrays, 1, per_home - 1, ORDER)
        head, coded = lax.optimization_barrier((head, coded))
        tail = send(coded, ORDER)
        return swap(partner, me, (1, per_home - 1), ORDER, (head, tail))

    z_lo, core = jnp.divmod(lax.axis_index("fsdp"), 2)
    swapped = lax.cond(
        lax.rem(z_lo + core, 2) == 0,
        late,
        early,
        partner, me, wg, wu, wd, gg, gu, gd,
    )
    mates = send(swapped, ORDER)
    partial = pl.pallas_call(
        functools.partial(squares_kernel, where),
        out_shape=jax.ShapeDtypeStruct((shards, 1, LANES), jnp.float32),
        in_specs=[vmem] * 4,
        out_specs=vmem,
        compiler_params=params,
        name="squares",
    )(mates, gg, gu, gd)
    sums = lax.all_to_all(partial, ("fsdp", "tp"), 0, 0, tiled=True)
    elements = tuple(shards * w.shape[1] * w.shape[2] for w in (wg, wu, wd))
    arrays = [jax.ShapeDtypeStruct(a.shape, jnp.float32) for a in (wg, wu, wd, mg, mu, md)]
    return pl.pallas_call(
        functools.partial(update_kernel, where, elements),
        out_shape=arrays,
        in_specs=[vmem] * 11,
        out_specs=[pl.BlockSpec(memory_space=pl.ANY)] * 6,
        scratch_shapes=[pltpu.VMEM(a.shape, a.dtype) for a in arrays] + [pltpu.SemaphoreType.DMA((6,))],
        compiler_params=params,
        name="update",
    )(sums, mates, wg, wu, wd, mg, mu, md, gg, gu, gd)


def solution(mesh):
    spec = P("rep", "fsdp", "tp")
    return jax.shard_map(
        local,
        mesh=mesh,
        in_specs=(P(),) + (spec,) * 9,
        out_specs=(spec,) * 6,
        check_vma=False,
    )
```

```python
import functools

import jax
import jax.numpy as jnp
from jax import lax
from jax.experimental import pallas as pl
from jax.experimental.pallas import tpu as pltpu
from jax.sharding import PartitionSpec as P

CLIP_RATIO = 0.5
BETA = 0.9
GAMMA = 0.4
RATE = 0.7
EPS = 1e-06

LANES = 128
TOP = 32767.0
STEPS = 16.0
TINY = 2.0**-120
REPLICAS = 16
ORDER = 10
VMEM_LIMIT = 24 * 1024 * 1024
ENCODE_LIMIT = 60 * 1024 * 1024


def plan(widths, replicas):
    counts = [width // LANES for width in widths]
    last = [(2, kind, c) for kind in range(2) for c in range(counts[2])]
    rest = [(slot, kind, c) for slot in range(2) for kind in range(2) for c in range(counts[slot])]
    rest += last[replicas:]
    bounds = (2 * counts[0], 2 * counts[0] + 2 * counts[1], len(rest))
    rest += [(slot, 2, 0) for slot in range(3)]
    more = -(-len(rest) // replicas)
    where = {tile: (i, 0) for i, tile in enumerate(last[:replicas])}
    where.update({tile: (i // more, 1 + i % more) for i, tile in enumerate(rest)})
    spare = [(i // more, 1 + i % more) for i in range(len(rest), more * replicas)]
    return where, spare, bounds, 1 + more


def place_of(order, index):
    return (order + REPLICAS - index) % REPLICAS


def groups_of(order):
    return [[place_of(order, i) for i in range(REPLICAS)]]


def exponent(peak):
    power = jnp.ceil(STEPS * jnp.log2(jnp.maximum(peak, TINY)))
    return jnp.clip(power, -120.0 * STEPS, 128.0 * STEPS - 1.0)


def encode_kernel(where, spare, first, count, order, names, *refs):
    n = len(names)
    srcs, out, dsts, sems = refs[:n], refs[n], refs[n + 1 : 2 * n + 1], refs[2 * n + 1]
    rows = srcs[0].shape[1]
    copies = [pltpu.make_async_copy(srcs[i], dsts[i], sems.at[i]) for i in range(n)]
    for copy in copies:
        copy.start()

    def put(at, value):
        home, place = at
        if first <= place < first + count:
            out[place_of(order, home), (place - first) * rows : (place - first + 1) * rows, :] = value

    for at in spare:
        put(at, jnp.zeros((rows, LANES), jnp.int16))
    powers = {}
    for (slot, kind), ref, copy in zip(names, dsts, copies):
        copy.wait()
        tiles = ref.shape[2] // LANES
        peak = jnp.abs(ref[0, :, 0:LANES])
        for c in range(1, tiles):
            peak = jnp.maximum(peak, jnp.abs(ref[0, :, c * LANES : (c + 1) * LANES]))
        power = exponent(jnp.max(peak.astype(jnp.float32), axis=(0, 1), keepdims=True))
        factor = jnp.broadcast_to(TOP * jnp.exp2(power * (-0.5 / STEPS)), (rows, LANES))
        for c in range(tiles):
            at = where[slot, kind, c]
            if first <= at[1] < first + count:
                x = ref[0, :, c * LANES : (c + 1) * LANES].astype(jnp.float32)
                level = x * lax.rsqrt(jnp.maximum(jnp.abs(x), TINY)) * factor
                level = jnp.round(jnp.clip(level, -TOP, TOP))
                put(at, level.astype(jnp.int32).astype(jnp.int16))
        powers[slot, kind] = jnp.broadcast_to(power, (rows, LANES)).astype(jnp.int32)
    if first + count > 1:
        upper = lax.broadcasted_iota(jnp.int32, (rows, LANES), 0) < 8
        for slot in range(3):
            put(where[slot, 2, 0], jnp.where(upper, powers[slot, 0], powers[slot, 1]).astype(jnp.int16))


def swap_kernel(bounds, cuts, rows, order, partner_hbm, me, *refs):
    inps, (out, partner, sem) = refs[: len(cuts)], refs[len(cuts) :]
    fetch = pltpu.make_async_copy(partner_hbm, partner, sem)
    fetch.start()
    fetch.wait()
    replicas = out.shape[0]
    more = sum(cuts) - 1
    for place in range(1 + more):
        slot = 2
        if place:
            tile = me[0] * more + place - 1
            slot = jnp.where(tile < bounds[0], 0, jnp.where(tile < bounds[1], 1, 2))
            slot = jnp.where(tile == bounds[2], 0, jnp.where(tile == bounds[2] + 1, 1, slot))
        inp, at = locate(inps, cuts, place)
        for r in range(replicas):
            source = place_of(order, partner[slot, r])
            out[place_of(ORDER, r), place * rows : (place + 1) * rows, :] = inp[source, at * rows : (at + 1) * rows, :]


def locate(parts, cuts, place):
    for part, cut in zip(parts, cuts):
        if place < cut:
            return part, place
        place -= cut
    raise ValueError("place")


def reader(where, rows, payload):
    def get(*tile):
        home, place = where[tile]
        return payload[place_of(ORDER, home), place * rows : (place + 1) * rows, :].astype(jnp.int32).astype(jnp.float32)

    return get


def decoded(code, scale):
    a = code * (1.0 / TOP)
    return a * jnp.abs(a) * scale


def scales_of(get, slot):
    power = jnp.exp2(get(slot, 2, 0) * (1.0 / STEPS))
    return power[0:1, :], power[8:9, :]


def squares_kernel(where, payload, gg, gu, gd, out):
    rows = gg.shape[1]
    get = reader(where, rows, payload)
    lane = lax.broadcasted_iota(jnp.int32, (1, LANES), 1)
    total = jnp.zeros((1, LANES), jnp.float32)
    for slot, g in enumerate((gg, gu, gd)):
        _, scale = scales_of(get, slot)
        sums = jnp.zeros((rows, LANES), jnp.float32)
        for c in range(g.shape[2] // LANES):
            own = g[0, :, c * LANES : (c + 1) * LANES].astype(jnp.float32)
            mixed = 0.5 * (own + decoded(get(slot, 1, c), scale))
            sums = sums + mixed * mixed
        total = jnp.where(lane == slot, jnp.sum(sums, axis=(0, 1), keepdims=True), total)
    out[...] = jnp.broadcast_to(total[None], out.shape)


def update_kernel(where, elements, sums, payload, wg, wu, wd, mg, mu, md, gg, gu, gd, *refs):
    outs, (og, ou, od, ng, nu, nd), sems = refs[:6], refs[6:12], refs[12]
    copies = [pltpu.make_async_copy(src, dst, sems.at[i]) for i, (src, dst) in enumerate(zip(refs[6:12], outs))]
    rows = gg.shape[1]
    get = reader(where, rows, payload)
    lane = lax.broadcasted_iota(jnp.int32, (1, LANES), 1)
    totals = jnp.sum(sums[...], axis=0)
    groups = ((wg, mg, gg, og, ng), (wu, mu, gu, ou, nu), (wd, md, gd, od, nd))
    for slot, (w, m, g, o, n) in enumerate(groups):
        scale_w, scale_g = scales_of(get, slot)
        squares = jnp.sum(jnp.where(lane == slot, totals, 0.0), axis=(0, 1), keepdims=True)
        bound = CLIP_RATIO * float(elements[slot]) ** 0.5
        clip = jnp.broadcast_to(jnp.minimum(1.0, bound / jnp.sqrt(squares + EPS)), (rows, LANES))
        for c in range(w.shape[2] // LANES):
            part = slice(c * LANES, (c + 1) * LANES)
            own = g[0, :, part].astype(jnp.float32)
            mixed = 0.5 * (own + decoded(get(slot, 1, c), scale_g))
            mate = decoded(get(slot, 0, c), scale_w)
            scaled = clip * mixed
            moment = BETA * m[0, :, part] + scaled
            weight = w[0, :, part]
            n[0, :, part] = moment
            o[0, :, part] = weight - GAMMA * (weight - mate) - RATE * (scaled + BETA * moment)
        copies[slot].start()
        copies[3 + slot].start()
    for copy in copies:
        copy.wait()


def local(partner, wg, wu, wd, mg, mu, md, gg, gu, gd):
    replicas = lax.axis_size("rep")
    shards = lax.axis_size("fsdp") * lax.axis_size("tp")
    rows = wg.shape[1]
    where, spare, bounds, per_home = plan((wg.shape[2], wu.shape[2], wd.shape[2]), replicas)
    params = pltpu.CompilerParams(vmem_limit_bytes=VMEM_LIMIT)
    vmem = pl.BlockSpec(memory_space=pltpu.VMEM)
    smem = pl.BlockSpec(memory_space=pltpu.SMEM)
    packed = jax.ShapeDtypeStruct((replicas, per_home * rows, LANES), jnp.int16)

    me = lax.axis_index("rep").reshape(1).astype(jnp.int32)

    def encode(arrays, first, count, order):
        return pl.pallas_call(
            functools.partial(encode_kernel, where, spare, first, count, order, tuple(arrays)),
            out_shape=jax.ShapeDtypeStruct((replicas, count * rows, LANES), jnp.int16),
            in_specs=[pl.BlockSpec(memory_space=pl.ANY)] * len(arrays),
            out_specs=vmem,
            scratch_shapes=[pltpu.VMEM(a.shape, a.dtype) for a in arrays.values()]
            + [pltpu.SemaphoreType.DMA((len(arrays),))],
            compiler_params=pltpu.CompilerParams(vmem_limit_bytes=ENCODE_LIMIT),
            name="encode",
        )(*arrays.values())

    def swap(partner, me, cuts, order, homed):
        return pl.pallas_call(
            functools.partial(swap_kernel, bounds, cuts, rows, order),
            out_shape=packed,
            in_specs=[pl.BlockSpec(memory_space=pl.ANY), smem] + [vmem] * len(cuts),
            out_specs=vmem,
            scratch_shapes=[pltpu.SMEM(partner.shape, partner.dtype), pltpu.SemaphoreType.DMA],
            compiler_params=params,
            name="swap",
        )(partner, me, *homed)

    def named(wg, wu, wd, gg, gu, gd):
        return {(2, 0): wd, (2, 1): gd, (0, 0): wg, (0, 1): gg, (1, 0): wu, (1, 1): gu}

    def send(payload, order):
        return lax.all_to_all(payload, "rep", 0, 0, tiled=True, axis_index_groups=groups_of(order))

    def early(partner, me, *arrays):
        coded = encode(named(*arrays), 0, per_home, ORDER)
        return swap(partner, me, (per_home,), ORDER, (send(coded, ORDER),))

    def late(partner, me, *arrays):
        named_arrays = named(*arrays)
        down = {key: a for key, a in named_arrays.items() if key[0] == 2}
        head = send(encode(down, 0, 1, ORDER), ORDER)
        coded = encode(named_arrays, 1, per_home - 1, ORDER)
        head, coded = lax.optimization_barrier((head, coded))
        tail = send(coded, ORDER)
        return swap(partner, me, (1, per_home - 1), ORDER, (head, tail))

    z_lo, core = jnp.divmod(lax.axis_index("fsdp"), 2)
    swapped = lax.cond(
        lax.rem(z_lo + core, 2) == 0,
        late,
        early,
        partner, me, wg, wu, wd, gg, gu, gd,
    )
    mates = send(swapped, ORDER)
    partial = pl.pallas_call(
        functools.partial(squares_kernel, where),
        out_shape=jax.ShapeDtypeStruct((shards, 1, LANES), jnp.float32),
        in_specs=[vmem] * 4,
        out_specs=vmem,
        compiler_params=params,
        name="squares",
    )(mates, gg, gu, gd)
    sums = lax.all_to_all(partial, ("fsdp", "tp"), 0, 0, tiled=True)
    elements = tuple(shards * w.shape[1] * w.shape[2] for w in (wg, wu, wd))
    arrays = [jax.ShapeDtypeStruct(a.shape, jnp.float32) for a in (wg, wu, wd, mg, mu, md)]
    return pl.pallas_call(
        functools.partial(update_kernel, where, elements),
        out_shape=arrays,
        in_specs=[vmem] * 11,
        out_specs=[pl.BlockSpec(memory_space=pl.ANY)] * 6,
        scratch_shapes=[pltpu.VMEM(a.shape, a.dtype) for a in arrays] + [pltpu.SemaphoreType.DMA((6,))],
        compiler_params=params,
        name="update",
    )(sums, mates, wg, wu, wd, mg, mu, md, gg, gu, gd)


def solution(mesh):
    spec = P("rep", "fsdp", "tp")
    return jax.shard_map(
        local,
        mesh=mesh,
        in_specs=(P(),) + (spec,) * 9,
        out_specs=(spec,) * 6,
        check_vma=False,
    )
```

```python
import functools

import jax
import jax.numpy as jnp
from jax import lax
from jax.experimental import pallas as pl
from jax.experimental.pallas import tpu as pltpu
from jax.sharding import PartitionSpec as P

CLIP_RATIO = 0.5
BETA = 0.9
GAMMA = 0.4
RATE = 0.7
EPS = 1e-06

LANES = 128
TOP = 32767.0
STEPS = 16.0
TINY = 2.0**-120
REPLICAS = 16
ORDER = 12
VMEM_LIMIT = 24 * 1024 * 1024
ENCODE_LIMIT = 60 * 1024 * 1024


def plan(widths, replicas):
    counts = [width // LANES for width in widths]
    last = [(2, kind, c) for kind in range(2) for c in range(counts[2])]
    rest = [(slot, kind, c) for slot in range(2) for kind in range(2) for c in range(counts[slot])]
    rest += last[replicas:]
    bounds = (2 * counts[0], 2 * counts[0] + 2 * counts[1], len(rest))
    rest += [(slot, 2, 0) for slot in range(3)]
    more = -(-len(rest) // replicas)
    where = {tile: (i, 0) for i, tile in enumerate(last[:replicas])}
    where.update({tile: (i // more, 1 + i % more) for i, tile in enumerate(rest)})
    spare = [(i // more, 1 + i % more) for i in range(len(rest), more * replicas)]
    return where, spare, bounds, 1 + more


def place_of(order, index):
    return (order + REPLICAS - index) % REPLICAS


def groups_of(order):
    return [[place_of(order, i) for i in range(REPLICAS)]]


def exponent(peak):
    power = jnp.ceil(STEPS * jnp.log2(jnp.maximum(peak, TINY)))
    return jnp.clip(power, -120.0 * STEPS, 128.0 * STEPS - 1.0)


def encode_kernel(where, spare, first, count, order, names, *refs):
    n = len(names)
    srcs, out, dsts, sems = refs[:n], refs[n], refs[n + 1 : 2 * n + 1], refs[2 * n + 1]
    rows = srcs[0].shape[1]
    copies = [pltpu.make_async_copy(srcs[i], dsts[i], sems.at[i]) for i in range(n)]
    for copy in copies:
        copy.start()

    def put(at, value):
        home, place = at
        if first <= place < first + count:
            out[place_of(order, home), (place - first) * rows : (place - first + 1) * rows, :] = value

    for at in spare:
        put(at, jnp.zeros((rows, LANES), jnp.int16))
    powers = {}
    for (slot, kind), ref, copy in zip(names, dsts, copies):
        copy.wait()
        tiles = ref.shape[2] // LANES
        peak = jnp.abs(ref[0, :, 0:LANES])
        for c in range(1, tiles):
            peak = jnp.maximum(peak, jnp.abs(ref[0, :, c * LANES : (c + 1) * LANES]))
        power = exponent(jnp.max(peak.astype(jnp.float32), axis=(0, 1), keepdims=True))
        factor = jnp.broadcast_to(TOP * jnp.exp2(power * (-0.5 / STEPS)), (rows, LANES))
        for c in range(tiles):
            at = where[slot, kind, c]
            if first <= at[1] < first + count:
                x = ref[0, :, c * LANES : (c + 1) * LANES].astype(jnp.float32)
                level = x * lax.rsqrt(jnp.maximum(jnp.abs(x), TINY)) * factor
                level = jnp.round(jnp.clip(level, -TOP, TOP))
                put(at, level.astype(jnp.int32).astype(jnp.int16))
        powers[slot, kind] = jnp.broadcast_to(power, (rows, LANES)).astype(jnp.int32)
    if first + count > 1:
        upper = lax.broadcasted_iota(jnp.int32, (rows, LANES), 0) < 8
        for slot in range(3):
            put(where[slot, 2, 0], jnp.where(upper, powers[slot, 0], powers[slot, 1]).astype(jnp.int16))


def swap_kernel(bounds, cuts, rows, order, partner_hbm, me, *refs):
    inps, (out, partner, sem) = refs[: len(cuts)], refs[len(cuts) :]
    fetch = pltpu.make_async_copy(partner_hbm, partner, sem)
    fetch.start()
    fetch.wait()
    replicas = out.shape[0]
    more = sum(cuts) - 1
    for place in range(1 + more):
        slot = 2
        if place:
            tile = me[0] * more + place - 1
            slot = jnp.where(tile < bounds[0], 0, jnp.where(tile < bounds[1], 1, 2))
            slot = jnp.where(tile == bounds[2], 0, jnp.where(tile == bounds[2] + 1, 1, slot))
        inp, at = locate(inps, cuts, place)
        for r in range(replicas):
            source = place_of(order, partner[slot, r])
            out[place_of(ORDER, r), place * rows : (place + 1) * rows, :] = inp[source, at * rows : (at + 1) * rows, :]


def locate(parts, cuts, place):
    for part, cut in zip(parts, cuts):
        if place < cut:
            return part, place
        place -= cut
    raise ValueError("place")


def reader(where, rows, payload):
    def get(*tile):
        home, place = where[tile]
        return payload[place_of(ORDER, home), place * rows : (place + 1) * rows, :].astype(jnp.int32).astype(jnp.float32)

    return get


def decoded(code, scale):
    a = code * (1.0 / TOP)
    return a * jnp.abs(a) * scale


def scales_of(get, slot):
    power = jnp.exp2(get(slot, 2, 0) * (1.0 / STEPS))
    return power[0:1, :], power[8:9, :]


def squares_kernel(where, payload, gg, gu, gd, out):
    rows = gg.shape[1]
    get = reader(where, rows, payload)
    lane = lax.broadcasted_iota(jnp.int32, (1, LANES), 1)
    total = jnp.zeros((1, LANES), jnp.float32)
    for slot, g in enumerate((gg, gu, gd)):
        _, scale = scales_of(get, slot)
        sums = jnp.zeros((rows, LANES), jnp.float32)
        for c in range(g.shape[2] // LANES):
            own = g[0, :, c * LANES : (c + 1) * LANES].astype(jnp.float32)
            mixed = 0.5 * (own + decoded(get(slot, 1, c), scale))
            sums = sums + mixed * mixed
        total = jnp.where(lane == slot, jnp.sum(sums, axis=(0, 1), keepdims=True), total)
    out[...] = jnp.broadcast_to(total[None], out.shape)


def update_kernel(where, elements, sums, payload, wg, wu, wd, mg, mu, md, gg, gu, gd, *refs):
    outs, (og, ou, od, ng, nu, nd), sems = refs[:6], refs[6:12], refs[12]
    copies = [pltpu.make_async_copy(src, dst, sems.at[i]) for i, (src, dst) in enumerate(zip(refs[6:12], outs))]
    rows = gg.shape[1]
    get = reader(where, rows, payload)
    lane = lax.broadcasted_iota(jnp.int32, (1, LANES), 1)
    totals = jnp.sum(sums[...], axis=0)
    groups = ((wg, mg, gg, og, ng), (wu, mu, gu, ou, nu), (wd, md, gd, od, nd))
    for slot, (w, m, g, o, n) in enumerate(groups):
        scale_w, scale_g = scales_of(get, slot)
        squares = jnp.sum(jnp.where(lane == slot, totals, 0.0), axis=(0, 1), keepdims=True)
        bound = CLIP_RATIO * float(elements[slot]) ** 0.5
        clip = jnp.broadcast_to(jnp.minimum(1.0, bound / jnp.sqrt(squares + EPS)), (rows, LANES))
        for c in range(w.shape[2] // LANES):
            part = slice(c * LANES, (c + 1) * LANES)
            own = g[0, :, part].astype(jnp.float32)
            mixed = 0.5 * (own + decoded(get(slot, 1, c), scale_g))
            mate = decoded(get(slot, 0, c), scale_w)
            scaled = clip * mixed
            moment = BETA * m[0, :, part] + scaled
            weight = w[0, :, part]
            n[0, :, part] = moment
            o[0, :, part] = weight - GAMMA * (weight - mate) - RATE * (scaled + BETA * moment)
        copies[slot].start()
        copies[3 + slot].start()
    for copy in copies:
        copy.wait()


def local(partner, wg, wu, wd, mg, mu, md, gg, gu, gd):
    replicas = lax.axis_size("rep")
    shards = lax.axis_size("fsdp") * lax.axis_size("tp")
    rows = wg.shape[1]
    where, spare, bounds, per_home = plan((wg.shape[2], wu.shape[2], wd.shape[2]), replicas)
    params = pltpu.CompilerParams(vmem_limit_bytes=VMEM_LIMIT)
    vmem = pl.BlockSpec(memory_space=pltpu.VMEM)
    smem = pl.BlockSpec(memory_space=pltpu.SMEM)
    packed = jax.ShapeDtypeStruct((replicas, per_home * rows, LANES), jnp.int16)

    me = lax.axis_index("rep").reshape(1).astype(jnp.int32)

    def encode(arrays, first, count, order):
        return pl.pallas_call(
            functools.partial(encode_kernel, where, spare, first, count, order, tuple(arrays)),
            out_shape=jax.ShapeDtypeStruct((replicas, count * rows, LANES), jnp.int16),
            in_specs=[pl.BlockSpec(memory_space=pl.ANY)] * len(arrays),
            out_specs=vmem,
            scratch_shapes=[pltpu.VMEM(a.shape, a.dtype) for a in arrays.values()]
            + [pltpu.SemaphoreType.DMA((len(arrays),))],
            compiler_params=pltpu.CompilerParams(vmem_limit_bytes=ENCODE_LIMIT),
            name="encode",
        )(*arrays.values())

    def swap(partner, me, cuts, order, homed):
        return pl.pallas_call(
            functools.partial(swap_kernel, bounds, cuts, rows, order),
            out_shape=packed,
            in_specs=[pl.BlockSpec(memory_space=pl.ANY), smem] + [vmem] * len(cuts),
            out_specs=vmem,
            scratch_shapes=[pltpu.SMEM(partner.shape, partner.dtype), pltpu.SemaphoreType.DMA],
            compiler_params=params,
            name="swap",
        )(partner, me, *homed)

    def named(wg, wu, wd, gg, gu, gd):
        return {(2, 0): wd, (2, 1): gd, (0, 0): wg, (0, 1): gg, (1, 0): wu, (1, 1): gu}

    def send(payload, order):
        return lax.all_to_all(payload, "rep", 0, 0, tiled=True, axis_index_groups=groups_of(order))

    def early(partner, me, *arrays):
        coded = encode(named(*arrays), 0, per_home, ORDER)
        return swap(partner, me, (per_home,), ORDER, (send(coded, ORDER),))

    def late(partner, me, *arrays):
        named_arrays = named(*arrays)
        down = {key: a for key, a in named_arrays.items() if key[0] == 2}
        head = send(encode(down, 0, 1, ORDER), ORDER)
        coded = encode(named_arrays, 1, per_home - 1, ORDER)
        head, coded = lax.optimization_barrier((head, coded))
        tail = send(coded, ORDER)
        return swap(partner, me, (1, per_home - 1), ORDER, (head, tail))

    z_lo, core = jnp.divmod(lax.axis_index("fsdp"), 2)
    swapped = lax.cond(
        lax.rem(z_lo + core, 2) == 0,
        late,
        early,
        partner, me, wg, wu, wd, gg, gu, gd,
    )
    mates = send(swapped, ORDER)
    partial = pl.pallas_call(
        functools.partial(squares_kernel, where),
        out_shape=jax.ShapeDtypeStruct((shards, 1, LANES), jnp.float32),
        in_specs=[vmem] * 4,
        out_specs=vmem,
        compiler_params=params,
        name="squares",
    )(mates, gg, gu, gd)
    sums = lax.all_to_all(partial, ("fsdp", "tp"), 0, 0, tiled=True)
    elements = tuple(shards * w.shape[1] * w.shape[2] for w in (wg, wu, wd))
    arrays = [jax.ShapeDtypeStruct(a.shape, jnp.float32) for a in (wg, wu, wd, mg, mu, md)]
    return pl.pallas_call(
        functools.partial(update_kernel, where, elements),
        out_shape=arrays,
        in_specs=[vmem] * 11,
        out_specs=[pl.BlockSpec(memory_space=pl.ANY)] * 6,
        scratch_shapes=[pltpu.VMEM(a.shape, a.dtype) for a in arrays] + [pltpu.SemaphoreType.DMA((6,))],
        compiler_params=params,
        name="update",
    )(sums, mates, wg, wu, wd, mg, mu, md, gg, gu, gd)


def solution(mesh):
    spec = P("rep", "fsdp", "tp")
    return jax.shard_map(
        local,
        mesh=mesh,
        in_specs=(P(),) + (spec,) * 9,
        out_specs=(spec,) * 6,
        check_vma=False,
    )
```
